512 devices in a mesh: dp: 128 (over z, y, x_lo), tensor: 4 (over x_hi, core).
Axes of the slice: x: 4 (x_hi: 2, x_lo: 2; x = x_hi * 2 + x_lo), y: 4, z: 16, core: 2. Of those that a mesh axis runs over, the one named last changes fastest.
Arguments:
- image_embed: bfloat16 [22528, 1152], P('dp', 'tensor'), may hold values from -8 to 8
- text_embed: bfloat16 [22528, 1152], P('dp', 'tensor'), may hold values from -8 to 8
- log_scale: float32 [1], replicated, may hold values from 3.7 to 4.6
- logit_bias: float32 [1], replicated, may hold values from -4 to -1
Outputs:
- grad_image: float32 [22528, 1152], P('dp', 'tensor')
- grad_text: float32 [22528, 1152], P('dp', 'tensor')
The draws below stay inside these ranges and needn't reach their ends.
All inputs are finite; a program needn't handle non-finite values.
Results may differ from the reference program's by a relative error of at most 0.0058.
Values may be sent and summed in bfloat16 or wider, within the bound.
A program may use at most 64 MiB of HBM per device.

```python
import math
import jax
import jax.numpy as jnp
from jax import lax

D = 1152
TOKENS = 22528


def shared_columns(key, lowest):
    spread = jax.random.uniform(key, (D,), jnp.float32)
    return jnp.exp(jnp.log(lowest) * (1.0 - spread))


def embed_draw(key, columns, row_lo, row_hi):
    base_key, row_key = jax.random.split(key)
    base = jnp.clip(jax.random.normal(base_key, (TOKENS, D), jnp.float32), -4.0, 4.0)
    row_spread = jax.random.uniform(row_key, (TOKENS, 1), jnp.float32)
    row_scale = jnp.exp(jnp.log(row_lo) + row_spread * (jnp.log(row_hi) - jnp.log(row_lo)))
    return (base * row_scale * columns[None, :]).astype(jnp.bfloat16)


def draw_image_embed(key, part):
    columns = shared_columns(key, 0.1)
    key = jax.random.fold_in(key, 11)
    return embed_draw(key, columns, 0.5, 2.0)


def draw_text_embed(key, part):
    columns = shared_columns(key, 0.1)
    key = jax.random.fold_in(key, 23)
    return embed_draw(key, columns, 0.5, 2.0)


def setup_inputs(seed: int = 0) -> dict:
    streams_of = jax.random.split(jax.random.key(seed), 5)
    image_embed = draw_image_embed(jax.random.fold_in(streams_of[4], 71), 0)
    text_embed = draw_text_embed(jax.random.fold_in(streams_of[4], 71), 0)
    log_scale = jnp.clip(jax.random.uniform(streams_of[2], (1,), jnp.float32, 3.7, 4.6), 3.7, 4.6)
    logit_bias = jnp.clip(jax.random.uniform(streams_of[3], (1,), jnp.float32, -4.0, -1.0), -4.0, -1.0)
    return {"image_embed": image_embed, "text_embed": text_embed, "log_scale": log_scale, "logit_bias": logit_bias}


def unit_rows(embed):
    values = embed.astype(jnp.float32)
    row_norm = jnp.sqrt(lax.optimization_barrier(jnp.sum(values * values, axis=1, keepdims=True)) + 1e-06)
    return (row_norm, values / row_norm)

def project_back(unit_grad, unit_vec, row_norm):
    inner = lax.optimization_barrier(jnp.sum(unit_vec * unit_grad, axis=1, keepdims=True))
    return (unit_grad - unit_vec * inner) / row_norm

def reference(image_embed, text_embed, log_scale, logit_bias):
    image_norm, image_unit = unit_rows(image_embed)
    text_norm, text_unit = unit_rows(text_embed)
    image_bf = image_unit.astype(jnp.bfloat16)
    text_bf = text_unit.astype(jnp.bfloat16)
    logit_scale = jnp.exp(log_scale[0])
    shift_value = logit_bias[0]
    block_rows = math.gcd(TOKENS, 512)
    block_count = TOKENS // block_rows

    def one_block(text_total, block_index):
        first_row = (block_index * block_rows).astype(jnp.int32)
        image_rows = lax.dynamic_slice_in_dim(image_bf, first_row, block_rows, 0)
        scores = lax.dot_general(image_rows, text_bf, (((1,), (1,)), ((), ())), preferred_element_type=jnp.float32)
        logits = logit_scale * scores + shift_value
        row_ids = first_row + jnp.arange(block_rows, dtype=jnp.int32)
        col_ids = jnp.arange(TOKENS, dtype=jnp.int32)
        identity = (row_ids[:, None] == col_ids[None, :]).astype(jnp.float32)
        pair_grad = (jax.nn.sigmoid(logits) - identity).astype(jnp.bfloat16)
        part_image = jnp.dot(pair_grad, text_bf, preferred_element_type=jnp.float32)
        part_text = lax.dot_general(pair_grad, image_rows, (((0,), (0,)), ((), ())), preferred_element_type=jnp.float32)
        return (text_total + part_text, part_image)
    text_sum, image_parts = lax.scan(one_block, jnp.zeros((TOKENS, D), jnp.float32), jnp.arange(block_count, dtype=jnp.int32))
    unit_grad_image = logit_scale * image_parts.reshape(TOKENS, D)
    unit_grad_text = logit_scale * text_sum
    grad_image = project_back(unit_grad_image, image_unit, image_norm)
    grad_text = project_back(unit_grad_text, text_unit, text_norm)
    return (grad_image, grad_text)
```

```python
import jax
import jax.numpy as jnp
from jax import lax
from jax.experimental import pallas as pl
from jax.experimental.pallas import tpu as pltpu
from jax.sharding import PartitionSpec as P

MESH = pl.DeviceIdType.MESH
BF = jnp.bfloat16
F32 = jnp.float32
NX, NY, NZ = 4, 4, 16
SHARD = 48
IMG_Z = (0, 1, -1, 2)
TXT_Z = (0, 8, 4, 12)
CHUNK = 256


def coords():
    dp, t = lax.axis_index("dp"), lax.axis_index("tensor")
    return (t // 2) * 2 + lax.rem(dp, 2), lax.rem(dp // 2, NY), dp // (2 * NY), lax.rem(t, 2)


def device(x, y, z, c):
    x, y, z = lax.rem(x + 2 * NX, NX), lax.rem(y + 2 * NY, NY), lax.rem(z + 2 * NZ, NZ)
    return (z * (2 * NY) + y * 2 + lax.rem(x, 2), (x // 2) * 2 + lax.rem(c, 2))


def at(slot, count=1):
    return pl.ds(slot * SHARD, count * SHARD)


def img_slot(g, d):
    return g * 4 + d


def txt_slot(g, core, d):
    return g * 8 + core * 4 + d


def kernel(
    scale_ref, bias_ref, img_in, txt_in, img_out, txt_out,
    block, raw, img, txt, img_grad, txt_grad,
    core_send, core_got, x_send, x_got, y_send, y_got, z_send, z_got, back,
    in_sem, gs, gr, rs, rr,
):
    x, y, z, c = coords()
    dp, t = lax.axis_index("dp"), lax.axis_index("tensor")
    quarter = block.shape[2]
    rows_in = img_in.shape[0]
    mirror = 1 - 2 * c

    loads = [
        pltpu.make_async_copy(ref, block.at[e, pl.ds(0, rows_in)], in_sem.at[e])
        for e, ref in enumerate((img_in, txt_in))
    ]
    for load in loads:
        load.start()
    for e in range(2):
        block[e, rows_in:, :] = jnp.zeros((block.shape[1] - rows_in, quarter), BF)

    peers = [(x, y, z + d, c) for d in (1, -1, 2, -2, 4, 8, 12)]
    peers += [(x, y + d, z, c) for d in (1, 2, 3)] + [(x + d, y, z, c) for d in (1, 2, 3)]
    peers += [(x, y, z, c + 1), (x + 2, y, z, c + 1)]
    barrier = pltpu.get_barrier_semaphore()
    for peer in peers:
        pl.semaphore_signal(barrier, inc=1, device_id=device(*peer), device_id_type=MESH)
    pl.semaphore_wait(barrier, len(peers))

    sent = []

    def go(copy):
        copy.start()
        sent.append(copy)

    def remote(src, dst, sems, index, to):
        return pltpu.make_async_remote_copy(
            src_ref=src, dst_ref=dst, send_sem=sems[0].at[index], recv_sem=sems[1].at[index],
            device_id=to, device_id_type=MESH,
        )

    gather, reduce = (gs, gr), (rs, rr)

    def swap(e, j):
        to = lax.rem(t + j, 4)
        rows = pl.ds(pl.multiple_of(to * SHARD, SHARD), SHARD)
        return remote(block.at[e, rows], raw.at[e, t], gather, e * 3 + j - 1, (dp, to))

    for e in (1, 0):
        loads[e].wait()
        for j in (2, 3, 1):
            go(swap(e, j))
        raw[e, t] = block[e, pl.ds(pl.multiple_of(t * SHARD, SHARD), SHARD), :]

    def unit(e):
        rows = jnp.concatenate([raw[e, q].astype(F32) for q in range(4)], axis=1)
        norm = jnp.sqrt(jnp.sum(rows * rows, axis=1, keepdims=True) + 1e-06)
        return rows / norm, norm

    def txt_z(g):
        to = device(x, y, z + TXT_Z[g], c)
        return remote(txt.at[at(0)], txt.at[at(txt_slot(g, 0, 0))], gather, 5 + g, to)

    def txt_x(g, d):
        to = device(x + d, y, z, c)
        return remote(txt.at[at(txt_slot(g, 0, 0))], txt.at[at(txt_slot(g, 0, d))], gather, 8 + g * 3 + d, to)

    def txt_core(g, d):
        to = device(x, y, z, c + 1)
        return remote(txt.at[at(txt_slot(g, 0, d))], txt.at[at(txt_slot(g, 1, d))], gather, 21 + g * 4 + d, to)

    def img_z(g):
        to = device(x, y, z + IMG_Z[g] * mirror, c)
        return remote(img.at[at(0)], img.at[at(img_slot(g, 0))], gather, 36 + g, to)

    def img_y(g, d):
        to = device(x, y + d, z, c)
        return remote(img.at[at(img_slot(g, 0))], img.at[at(img_slot(g, d))], gather, 39 + g * 3 + d, to)

    for j in (1, 2, 3):
        swap(1, j).wait_recv()
    txt[at(0), :] = unit(1)[0].astype(BF)
    for g in (1, 2, 3):
        go(txt_z(g))
    for d in (2, 1, 3):
        go(txt_x(0, d))
    go(txt_core(0, 0))
    for j in (1, 2, 3):
        swap(0, j).wait_recv()
    img[at(0), :] = unit(0)[0].astype(BF)
    for g in (3, 1, 2):
        go(img_z(g))
    for d in (2, 1, 3):
        go(img_y(0, d))

    img_grad[...] = jnp.zeros_like(img_grad)
    txt_grad[...] = jnp.zeros_like(txt_grad)
    scale = jnp.exp(jnp.full((1, 1), scale_ref[0], F32))
    bias = bias_ref[0]

    def forward_x(g):
        txt_z(g).wait_recv()
        go(txt_core(g, 0))
        for d in (2, 1, 3):
            go(txt_x(g, d))

    def forward_core(g):
        for d in (1, 3, 2):
            txt_x(g, d).wait_recv()
            go(txt_core(g, d))

    def got_core(g):
        for d in range(4):
            txt_core(g, d).wait_recv()

    def pairs(g):
        here = at(txt_slot(g, 0, 0), 8)

        def step(k, carry):
            there = pl.ds(pl.multiple_of(k * CHUNK, CHUNK), CHUNK)
            scores = lax.dot_general(
                img[there, :], txt[here, :], (((1,), (1,)), ((), ())), preferred_element_type=F32
            )
            part = jax.nn.sigmoid(scale * scores + bias).astype(BF)
            img_grad[there, :] += jnp.dot(part, txt[here, :], preferred_element_type=F32)
            txt_grad[here, :] += lax.dot_general(
                part, img[there, :], (((0,), (0,)), ((), ())), preferred_element_type=F32
            )
            return carry

        lax.fori_loop(0, img.shape[0] // CHUNK, step, 0)

    def cut_core(g):
        to = device(x, y, z, c + 1)
        return remote(core_send.at[g], core_got.at[g], reduce, g, to)

    def cut_x(g, d):
        to = device(x - d, y, z, c)
        return remote(x_send.at[g, d - 1], x_got.at[g, d - 1], reduce, 3 + g * 3 + d, to)

    def cut_y(g, d):
        to = device(x, y - d, z, c)
        return remote(y_send.at[g, d - 1], y_got.at[g, d - 1], reduce, 15 + g * 3 + d, to)

    def cut_z(e, g):
        to = device(x, y, z - (TXT_Z[g] if e else IMG_Z[g] * mirror), c)
        return remote(z_send.at[e, g - 1], z_got.at[e, g - 1], reduce, 27 + e * 3 + g, to)

    def give_core(g):
        core_send[g] = txt_grad[at(txt_slot(g, 1, 0), 4), :].astype(BF)
        go(cut_core(g))

    def give_x(g):
        cut_core(g).wait_recv()
        for d in (2, 1, 3):
            mine = txt_grad[at(txt_slot(g, 0, d)), :]
            x_send[g, d - 1] = (mine + core_got[g, at(d), :].astype(F32)).astype(BF)
            go(cut_x(g, d))
        return None

    def txt_total(g):
        total = txt_grad[at(txt_slot(g, 0, 0)), :] + core_got[g, at(0), :].astype(F32)
        for d in (1, 3, 2):
            cut_x(g, d).wait_recv()
            total += x_got[g, d - 1].astype(F32)
        return total

    def img_total(g):
        total = img_grad[at(img_slot(g, 0)), :]
        for d in (1, 3, 2):
            cut_y(g, d).wait_recv()
            total += y_got[g, d - 1].astype(F32)
        return total

    def give_z(e, g):
        z_send[e, g - 1] = (txt_total(g) if e else img_total(g)).astype(BF)
        go(cut_z(e, g))

    def swap_back(e, j):
        to = lax.rem(t + j, 4)
        out = (img_out, txt_out)[e]
        rows = pl.ds(pl.multiple_of(t * SHARD, SHARD), SHARD)
        return remote(back.at[e, to], out.at[rows], reduce, 34 + e * 3 + j - 1, (dp, to))

    def finish(e):
        total = txt_total(0) if e else img_total(0)
        for g in (1, 2, 3):
            cut_z(e, g).wait_recv()
            total += z_got[e, g - 1].astype(F32)
        rows, norm = unit(e)
        own = (txt, img)[e][at(0), :].astype(F32)
        grad = scale * (total - own)
        inner = jnp.sum(rows * grad, axis=1, keepdims=True)
        grad = ((grad - rows * inner) / norm).astype(BF)
        for q in range(4):
            back[e, q] = grad[:, q * quarter : (q + 1) * quarter]
        for j in (2, 3, 1):
            go(swap_back(e, j))
        keep = pltpu.make_async_copy(
            back.at[e, t], (img_out, txt_out)[e].at[pl.ds(pl.multiple_of(t * SHARD, SHARD), SHARD)], in_sem.at[e]
        )
        keep.start()
        return keep

    forward_core(0)
    for g in (1, 2, 3):
        img_z(g).wait_recv()
        for d in (2, 1, 3):
            go(img_y(g, d))
    for g in range(4):
        for d in (1, 2, 3):
            img_y(g, d).wait_recv()
    got_core(0)
    pairs(0)
    give_core(0)
    forward_x(2)
    forward_x(3)
    forward_core(2)
    forward_core(3)
    got_core(2)
    pairs(2)
    give_core(2)
    give_x(0)
    forward_x(1)
    got_core(3)
    pairs(3)
    give_core(3)
    give_x(2)
    forward_core(1)
    give_z(1, 2)
    give_x(3)
    got_core(1)
    pairs(1)
    give_core(1)
    for g in (3, 1, 2, 0):
        for d in (2, 1, 3):
            y_send[g, d - 1] = img_grad[at(img_slot(g, d)), :].astype(BF)
            go(cut_y(g, d))
    give_x(1)
    give_z(1, 3)
    for g in (3, 1, 2):
        give_z(0, g)
    give_z(1, 1)
    keep = [finish(0), finish(1)]
    for e in range(2):
        for j in (1, 2, 3):
            swap_back(e, j).wait_recv()
        keep[e].wait()
    for copy in sent:
        copy.wait_send()


def body(image_embed, text_embed, log_scale, logit_bias):
    rows, quarter = image_embed.shape
    width = 4 * quarter
    padded = 4 * SHARD
    vmem = pltpu.VMEM
    outs = pl.pallas_call(
        kernel,
        out_shape=[jax.ShapeDtypeStruct((padded, quarter), BF)] * 2,
        in_specs=[pl.BlockSpec(memory_space=pltpu.SMEM)] * 2 + [pl.BlockSpec(memory_space=pl.ANY)] * 2,
        out_specs=[pl.BlockSpec(memory_space=pl.ANY)] * 2,
        scratch_shapes=[
            vmem((2, padded, quarter), BF),
            vmem((2, 4, SHARD, quarter), BF),
            vmem((16 * SHARD, width), BF),
            vmem((32 * SHARD, width), BF),
            vmem((16 * SHARD, width), F32),
            vmem((32 * SHARD, width), F32),
            vmem((4, 4 * SHARD, width), BF),
            vmem((4, 4 * SHARD, width), BF),
            vmem((4, 3, SHARD, width), BF),
            vmem((4, 3, SHARD, width), BF),
            vmem((4, 3, SHARD, width), BF),
            vmem((4, 3, SHARD, width), BF),
            vmem((2, 3, SHARD, width), BF),
            vmem((2, 3, SHARD, width), BF),
            vmem((2, 4, SHARD, quarter), BF),
            pltpu.SemaphoreType.DMA((2,)),
            pltpu.SemaphoreType.DMA((52,)),
            pltpu.SemaphoreType.DMA((52,)),
            pltpu.SemaphoreType.DMA((40,)),
            pltpu.SemaphoreType.DMA((40,)),
        ],
        compiler_params=pltpu.CompilerParams(
            collective_id=0, has_side_effects=True, vmem_limit_bytes=56 * 2**20
        ),
    )(log_scale, logit_bias, image_embed, text_embed)
    return tuple(out[:rows].astype(F32) for out in outs)


def solution(mesh):
    placed = (P("dp", "tensor"), P("dp", "tensor"), P(), P())
    return jax.shard_map(
        body,
        mesh=mesh,
        in_specs=placed,
        out_specs=(P("dp", "tensor"), P("dp", "tensor")),
        check_vma=False,
    )
```

```python
import jax
import jax.numpy as jnp
from jax import lax
from jax.experimental import pallas as pl
from jax.experimental.pallas import tpu as pltpu
from jax.sharding import PartitionSpec as P

MESH = pl.DeviceIdType.MESH
BF = jnp.bfloat16
F32 = jnp.float32
NX, NY, NZ = 4, 4, 16
SHARD = 48
IMG_Z = (0, 1, -1, 2)
TXT_Z = (0, 8, 4, 12)
CHUNK = 256


def coords():
    dp, t = lax.axis_index("dp"), lax.axis_index("tensor")
    return (t // 2) * 2 + lax.rem(dp, 2), lax.rem(dp // 2, NY), dp // (2 * NY), lax.rem(t, 2)


def device(x, y, z, c):
    x, y, z = lax.rem(x + 2 * NX, NX), lax.rem(y + 2 * NY, NY), lax.rem(z + 2 * NZ, NZ)
    return (z * (2 * NY) + y * 2 + lax.rem(x, 2), (x // 2) * 2 + lax.rem(c, 2))


def at(slot, count=1):
    return pl.ds(slot * SHARD, count * SHARD)


def img_slot(g, d):
    return (3 - g) * 4 + d


def txt_slot(g, core, d):
    return g * 8 + core * 4 + d


def kernel(
    scale_ref, bias_ref, img_in, txt_in, img_out, txt_out,
    block, raw, img, txt, img_grad, txt_grad,
    core_send, core_got, x_send, x_got, y_send, y_got, z_send, z_got, back,
    in_sem, gs, gr, rs, rr,
):
    x, y, z, c = coords()
    dp, t = lax.axis_index("dp"), lax.axis_index("tensor")
    quarter = block.shape[2]
    rows_in = img_in.shape[0]
    mirror = 1 - 2 * c

    loads = [
        pltpu.make_async_copy(ref, block.at[e, pl.ds(0, rows_in)], in_sem.at[e])
        for e, ref in enumerate((img_in, txt_in))
    ]
    for load in loads:
        load.start()
    for e in range(2):
        block[e, rows_in:, :] = jnp.zeros((block.shape[1] - rows_in, quarter), BF)

    peers = [(x, y, z + d, c) for d in (1, -1, 2, -2, 4, 8, 12)]
    peers += [(x, y + d, z, c) for d in (1, 2, 3)] + [(x + d, y, z, c) for d in (1, 2, 3)]
    peers += [(x, y, z, c + 1), (x + 2, y, z, c + 1)]
    barrier = pltpu.get_barrier_semaphore()
    for peer in peers:
        pl.semaphore_signal(barrier, inc=1, device_id=device(*peer), device_id_type=MESH)
    pl.semaphore_wait(barrier, len(peers))

    sent = []

    def go(copy):
        copy.start()
        sent.append(copy)

    def remote(src, dst, sems, index, to):
        return pltpu.make_async_remote_copy(
            src_ref=src, dst_ref=dst, send_sem=sems[0].at[index], recv_sem=sems[1].at[index],
            device_id=to, device_id_type=MESH,
        )

    gather, reduce = (gs, gr), (rs, rr)

    def swap(e, j):
        to = lax.rem(t + j, 4)
        rows = pl.ds(pl.multiple_of(to * SHARD, SHARD), SHARD)
        return remote(block.at[e, rows], raw.at[e, t], gather, e * 3 + j - 1, (dp, to))

    for e in (0, 1):
        loads[e].wait()
        for j in (2, 3, 1):
            go(swap(e, j))
        raw[e, t] = block[e, pl.ds(pl.multiple_of(t * SHARD, SHARD), SHARD), :]

    def unit(e):
        rows = jnp.concatenate([raw[e, q].astype(F32) for q in range(4)], axis=1)
        norm = jnp.sqrt(jnp.sum(rows * rows, axis=1, keepdims=True) + 1e-06)
        return rows / norm, norm

    def txt_z(g):
        to = device(x, y, z + TXT_Z[g], c)
        return remote(txt.at[at(0)], txt.at[at(txt_slot(g, 0, 0))], gather, 5 + g, to)

    def txt_x(g, d):
        to = device(x + d, y, z, c)
        return remote(txt.at[at(txt_slot(g, 0, 0))], txt.at[at(txt_slot(g, 0, d))], gather, 8 + g * 3 + d, to)

    def txt_core(g, d):
        to = device(x, y, z, c + 1)
        return remote(txt.at[at(txt_slot(g, 0, d))], txt.at[at(txt_slot(g, 1, d))], gather, 21 + g * 4 + d, to)

    def img_z(g):
        to = device(x, y, z + IMG_Z[g] * mirror, c)
        return remote(img.at[at(img_slot(0, 0))], img.at[at(img_slot(g, 0))], gather, 36 + g, to)

    def img_y(g, d):
        to = device(x, y + d, z, c)
        return remote(img.at[at(img_slot(g, 0))], img.at[at(img_slot(g, d))], gather, 39 + g * 3 + d, to)

    own_img, own_txt = at(img_slot(0, 0)), at(txt_slot(0, 0, 0))
    for j in (1, 3, 2):
        swap(0, j).wait_recv()
    img[own_img, :] = unit(0)[0].astype(BF)
    for g in (3, 1, 2):
        go(img_z(g))
    for d in (2, 1, 3):
        go(img_y(0, d))
    for j in (1, 3, 2):
        swap(1, j).wait_recv()
    txt[own_txt, :] = unit(1)[0].astype(BF)
    for g in (2, 3):
        txt_z(g).start()
    for d in (2, 1, 3):
        go(txt_x(0, d))
    go(txt_core(0, 0))

    img_grad[...] = jnp.zeros_like(img_grad)
    txt_grad[...] = jnp.zeros_like(txt_grad)
    scale = jnp.exp(jnp.full((1, 1), scale_ref[0], F32))
    bias = bias_ref[0]

    def forward_x(g):
        txt_z(g).wait_recv()
        go(txt_core(g, 0))
        for d in (2, 1, 3):
            go(txt_x(g, d))

    def forward_core(g):
        for d in (1, 3, 2):
            txt_x(g, d).wait_recv()
            go(txt_core(g, d))

    def got_core(g):
        for d in range(4):
            txt_core(g, d).wait_recv()

    def pairs_chunk(g, k):
        here = at(txt_slot(g, 0, 0), 8)
        there = pl.ds(k * CHUNK if isinstance(k, int) else pl.multiple_of(k * CHUNK, CHUNK), CHUNK)
        scores = lax.dot_general(
            img[there, :], txt[here, :], (((1,), (1,)), ((), ())), preferred_element_type=F32
        )
        part = jax.nn.sigmoid(scale * scores + bias).astype(BF)
        img_grad[there, :] += jnp.dot(part, txt[here, :], preferred_element_type=F32)
        txt_grad[here, :] += lax.dot_general(
            part, img[there, :], (((0,), (0,)), ((), ())), preferred_element_type=F32
        )

    def pairs(g):
        def step(k, carry):
            pairs_chunk(g, k)
            return carry

        lax.fori_loop(0, img.shape[0] // CHUNK, step, 0)

    def cut_core(g):
        to = device(x, y, z, c + 1)
        return remote(core_send.at[g], core_got.at[g], reduce, g, to)

    def cut_x(g, d):
        to = device(x - d, y, z, c)
        return remote(x_send.at[g, d - 1], x_got.at[g, d - 1], reduce, 3 + g * 3 + d, to)

    def cut_y(g, d):
        to = device(x, y - d, z, c)
        return remote(y_send.at[g, d - 1], y_got.at[g, d - 1], reduce, 15 + g * 3 + d, to)

    def cut_z(e, g):
        to = device(x, y, z - (TXT_Z[g] if e else IMG_Z[g] * mirror), c)
        return remote(z_send.at[e, g - 1], z_got.at[e, g - 1], reduce, 27 + e * 3 + g, to)

    def give_y(g, d):
        y_send[g, d - 1] = img_grad[at(img_slot(g, d)), :].astype(BF)
        go(cut_y(g, d))

    def give_core(g):
        core_send[g] = txt_grad[at(txt_slot(g, 1, 0), 4), :].astype(BF)
        go(cut_core(g))

    def give_x(g):
        cut_core(g).wait_recv()
        for d in (2, 1, 3):
            mine = txt_grad[at(txt_slot(g, 0, d)), :]
            x_send[g, d - 1] = (mine + core_got[g, at(d), :].astype(F32)).astype(BF)
            go(cut_x(g, d))
        return None

    def txt_total(g):
        total = txt_grad[at(txt_slot(g, 0, 0)), :] + core_got[g, at(0), :].astype(F32)
        for d in (1, 3, 2):
            cut_x(g, d).wait_recv()
            total += x_got[g, d - 1].astype(F32)
        return total

    def img_total(g):
        total = img_grad[at(img_slot(g, 0)), :]
        for d in (1, 3, 2):
            cut_y(g, d).wait_recv()
            total += y_got[g, d - 1].astype(F32)
        return total

    def give_z(e, g):
        z_send[e, g - 1] = (txt_total(g) if e else img_total(g)).astype(BF)
        go(cut_z(e, g))

    def swap_back(e, j):
        to = lax.rem(t + j, 4)
        out = (img_out, txt_out)[e]
        rows = pl.ds(pl.multiple_of(t * SHARD, SHARD), SHARD)
        return remote(back.at[e, to], out.at[rows], reduce, 34 + e * 3 + j - 1, (dp, to))

    def finish(e):
        total = txt_total(0) if e else img_total(0)
        for g in (1, 2, 3):
            cut_z(e, g).wait_recv()
            total += z_got[e, g - 1].astype(F32)
        rows, norm = unit(e)
        own = (txt[own_txt, :], img[own_img, :])[e].astype(F32)
        grad = scale * (total - own)
        inner = jnp.sum(rows * grad, axis=1, keepdims=True)
        grad = ((grad - rows * inner) / norm).astype(BF)
        for q in range(4):
            back[e, q] = grad[:, q * quarter : (q + 1) * quarter]
        for j in (2, 3, 1):
            go(swap_back(e, j))
        keep = pltpu.make_async_copy(
            back.at[e, t], (img_out, txt_out)[e].at[pl.ds(pl.multiple_of(t * SHARD, SHARD), SHARD)], in_sem.at[e]
        )
        keep.start()
        return keep

    for g in (1, 2, 3):
        img_z(g).wait_recv()
        for d in (2, 1, 3):
            go(img_y(g, d))
    forward_core(0)
    for g in (2, 3):
        txt_z(g).wait_send()
    go(txt_z(1))
    forward_x(2)
    forward_x(3)
    for g in range(4):
        for d in (1, 2, 3):
            img_y(g, d).wait_recv()
    got_core(0)
    pairs(0)
    give_core(0)
    forward_core(2)
    give_x(0)
    got_core(2)
    pairs(2)
    give_core(2)
    forward_core(3)
    forward_x(1)
    give_x(2)
    got_core(3)
    pairs(3)
    give_core(3)
    forward_core(1)
    give_z(1, 2)
    give_x(3)
    got_core(1)
    done = 0
    for k in range(img.shape[0] // CHUNK):
        pairs_chunk(1, k)
        if (k + 1) * CHUNK == img.shape[0]:
            give_core(1)
        for slot in range(done, (k + 1) * CHUNK // SHARD):
            if slot % 4:
                give_y(3 - slot // 4, slot % 4)
            done = slot + 1
    give_z(1, 3)
    give_x(1)
    for g in (3, 1, 2):
        give_z(0, g)
    give_z(1, 1)
    keep = [finish(0), finish(1)]
    for e in range(2):
        for j in (1, 2, 3):
            swap_back(e, j).wait_recv()
        keep[e].wait()
    for copy in sent:
        copy.wait_send()


def body(image_embed, text_embed, log_scale, logit_bias):
    rows, quarter = image_embed.shape
    width = 4 * quarter
    padded = 4 * SHARD
    vmem = pltpu.VMEM
    outs = pl.pallas_call(
        kernel,
        out_shape=[jax.ShapeDtypeStruct((padded, quarter), BF)] * 2,
        in_specs=[pl.BlockSpec(memory_space=pltpu.SMEM)] * 2 + [pl.BlockSpec(memory_space=pl.ANY)] * 2,
        out_specs=[pl.BlockSpec(memory_space=pl.ANY)] * 2,
        scratch_shapes=[
            vmem((2, padded, quarter), BF),
            vmem((2, 4, SHARD, quarter), BF),
            vmem((16 * SHARD, width), BF),
            vmem((32 * SHARD, width), BF),
            vmem((16 * SHARD, width), F32),
            vmem((32 * SHARD, width), F32),
            vmem((4, 4 * SHARD, width), BF),
            vmem((4, 4 * SHARD, width), BF),
            vmem((4, 3, SHARD, width), BF),
            vmem((4, 3, SHARD, width), BF),
            vmem((4, 3, SHARD, width), BF),
            vmem((4, 3, SHARD, width), BF),
            vmem((2, 3, SHARD, width), BF),
            vmem((2, 3, SHARD, width), BF),
            vmem((2, 4, SHARD, quarter), BF),
            pltpu.SemaphoreType.DMA((2,)),
            pltpu.SemaphoreType.DMA((52,)),
            pltpu.SemaphoreType.DMA((52,)),
            pltpu.SemaphoreType.DMA((40,)),
            pltpu.SemaphoreType.DMA((40,)),
        ],
        compiler_params=pltpu.CompilerParams(
            collective_id=0, has_side_effects=True, vmem_limit_bytes=56 * 2**20
        ),
    )(log_scale, logit_bias, image_embed, text_embed)
    return tuple(out[:rows].astype(F32) for out in outs)


def solution(mesh):
    placed = (P("dp", "tensor"), P("dp", "tensor"), P(), P())
    return jax.shard_map(
        body,
        mesh=mesh,
        in_specs=placed,
        out_specs=(P("dp", "tensor"), P("dp", "tensor")),
        check_vma=False,
    )
```

```python
import jax
import jax.numpy as jnp
from jax import lax
from jax.experimental import pallas as pl
from jax.experimental.pallas import tpu as pltpu
from jax.sharding import PartitionSpec as P

MESH = pl.DeviceIdType.MESH
BF = jnp.bfloat16
F32 = jnp.float32
NX, NY, NZ = 4, 4, 16
SHARD = 48
IMG_Z = (0, 1, -1, 2)
TXT_Z = (0, 8, 4, 12)
FIRST = 2
HALF = 640


def coords():
    dp, t = lax.axis_index("dp"), lax.axis_index("tensor")
    return (t // 2) * 2 + lax.rem(dp, 2), lax.rem(dp // 2, NY), dp // (2 * NY), lax.rem(t, 2)


def device(x, y, z, c):
    x, y, z = lax.rem(x + 2 * NX, NX), lax.rem(y + 2 * NY, NY), lax.rem(z + 2 * NZ, NZ)
    return (z * (2 * NY) + y * 2 + lax.rem(x, 2), (x // 2) * 2 + lax.rem(c, 2))


def at(slot, count=1):
    return pl.ds(slot * SHARD, count * SHARD)


def img_slot(g, d):
    return (3 - g) * 4 + d


def txt_slot(g, core, d):
    return g * 8 + core * 4 + d


def kernel(
    scale_in, bias_in, img_in, txt_in, img_out, txt_out,
    scale_ref, bias_ref, block, raw, img, txt, img_grad, txt_grad,
    core_send, core_got, x_send, x_got, y_send, y_got, z_send, z_got, back,
    in_sem, gs, gr, rs, rr,
):
    x, y, z, c = coords()
    dp, t = lax.axis_index("dp"), lax.axis_index("tensor")
    quarter = block.shape[2]
    rows_in = img_in.shape[0]
    mirror = 1 - 2 * c

    loads = [
        pltpu.make_async_copy(ref, block.at[e, pl.ds(0, rows_in)], in_sem.at[e])
        for e, ref in enumerate((img_in, txt_in))
    ]
    loads.append(pltpu.make_async_copy(scale_in, scale_ref, in_sem.at[2]))
    loads.append(pltpu.make_async_copy(bias_in, bias_ref, in_sem.at[3]))
    for load in loads:
        load.start()
    for e in range(2):
        block[e, rows_in:, :] = jnp.zeros((block.shape[1] - rows_in, quarter), BF)

    peers = [(x, y, z + d, c) for d in (1, -1, 2, -2, 4, 8, 12)]
    peers += [(x, y + d, z, c) for d in (1, 2, 3)] + [(x + d, y, z, c) for d in (1, 2, 3)]
    peers += [(x, y, z, c + 1), (x + 2, y, z, c + 1)]
    barrier = pltpu.get_barrier_semaphore()
    for peer in peers:
        pl.semaphore_signal(barrier, inc=1, device_id=device(*peer), device_id_type=MESH)
    pl.semaphore_wait(barrier, len(peers))

    sent = []

    def go(copy):
        copy.start()
        sent.append(copy)

    def remote(src, dst, sems, index, to):
        return pltpu.make_async_remote_copy(
            src_ref=src, dst_ref=dst, send_sem=sems[0].at[index], recv_sem=sems[1].at[index],
            device_id=to, device_id_type=MESH,
        )

    gather, reduce = (gs, gr), (rs, rr)

    def swap(e, j):
        to = lax.rem(t + j, 4)
        rows = pl.ds(pl.multiple_of(to * SHARD, SHARD), SHARD)
        return remote(block.at[e, rows], raw.at[e, t], gather, e * 3 + j - 1, (dp, to))

    for e in (0, 1):
        loads[e].wait()
        for j in (2, 3, 1):
            go(swap(e, j))
        raw[e, t] = block[e, pl.ds(pl.multiple_of(t * SHARD, SHARD), SHARD), :]

    def unit(e):
        rows = jnp.concatenate([raw[e, q].astype(F32) for q in range(4)], axis=1)
        norm = jnp.sqrt(jnp.sum(rows * rows, axis=1, keepdims=True) + 1e-06)
        return rows / norm, norm

    def txt_z(g):
        to = device(x, y, z + TXT_Z[g], c)
        return remote(txt.at[at(0)], txt.at[at(txt_slot(g, 0, 0))], gather, 5 + g, to)

    def txt_far(h):
        lanes = (pl.ds(0, HALF), pl.ds(HALF, txt.shape[1] - HALF))[h]
        to = device(x, y, z + (4, -4)[h], c)
        src, dst = txt.at[at(txt_slot(2 + h, 0, 0)), lanes], txt.at[at(txt_slot(1, 0, 0)), lanes]
        return remote(src, dst, gather, (6, 52)[h], to)

    def txt_x(g, d):
        to = device(x + d, y, z, c)
        return remote(txt.at[at(txt_slot(g, 0, 0))], txt.at[at(txt_slot(g, 0, d))], gather, 8 + g * 3 + d, to)

    def txt_core(g, d):
        to = device(x, y, z, c + 1)
        return remote(txt.at[at(txt_slot(g, 0, d))], txt.at[at(txt_slot(g, 1, d))], gather, 21 + g * 4 + d, to)

    def img_z(g):
        to = device(x, y, z + IMG_Z[g] * mirror, c)
        return remote(img.at[at(img_slot(0, 0))], img.at[at(img_slot(g, 0))], gather, 36 + g, to)

    def img_y(g, d):
        to = device(x, y + d, z, c)
        return remote(img.at[at(img_slot(g, 0))], img.at[at(img_slot(g, d))], gather, 39 + g * 3 + d, to)

    own_img, own_txt = at(img_slot(0, 0)), at(txt_slot(0, 0, 0))
    for j in (1, 3, 2):
        swap(0, j).wait_recv()
    img[own_img, :] = unit(0)[0].astype(BF)
    for g in (3, 1, 2):
        go(img_z(g))
    for d in (2, 1, 3):
        go(img_y(0, d))
    for j in (1, 3, 2):
        swap(1, j).wait_recv()
    txt[own_txt, :] = unit(1)[0].astype(BF)
    for g in (2, 3):
        go(txt_z(g))
    for d in (2, 1, 3):
        go(txt_x(0, d))
    go(txt_core(0, 0))

    for load in loads[2:]:
        load.wait()
    scale = jnp.exp(jnp.full((1, 1), scale_ref[0], F32))
    bias = bias_ref[0]

    def forward_x(g):
        if g == 1:
            txt_far(0).wait_recv()
            txt_far(1).wait_recv()
        else:
            txt_z(g).wait_recv()
            go(txt_far(g - 2))
        go(txt_core(g, 0))
        for d in (2, 1, 3):
            go(txt_x(g, d))

    def forward_core(g):
        for d in (1, 3, 2):
            txt_x(g, d).wait_recv()
            go(txt_core(g, d))

    def got_core(g):
        for d in range(4):
            txt_core(g, d).wait_recv()

    def pairs(g, first=0, count=16):
        here, there = at(txt_slot(g, 0, 0), 8), at(first, count)
        scores = lax.dot_general(
            img[there, :], txt[here, :], (((1,), (1,)), ((), ())), preferred_element_type=F32
        )
        part = jax.nn.sigmoid(scale * scores + bias).astype(BF)
        to_img = jnp.dot(part, txt[here, :], preferred_element_type=F32)
        if g == FIRST:
            img_grad[there, :] = to_img
        else:
            img_grad[there, :] += to_img
        to_txt = lax.dot_general(part, img[there, :], (((0,), (0,)), ((), ())), preferred_element_type=F32)
        if first == 0:
            txt_grad[here, :] = to_txt
        else:
            txt_grad[here, :] += to_txt

    def cut_core(g):
        to = device(x, y, z, c + 1)
        return remote(core_send.at[g], core_got.at[g], reduce, g, to)

    def cut_x(g, d):
        to = device(x - d, y, z, c)
        return remote(x_send.at[g, d - 1], x_got.at[g, d - 1], reduce, 3 + g * 3 + d, to)

    def cut_y(g, d):
        to = device(x, y - d, z, c)
        return remote(y_send.at[g, d - 1], y_got.at[g, d - 1], reduce, 15 + g * 3 + d, to)

    def cut_z(e, g):
        to = device(x, y, z - (TXT_Z[g] if e else IMG_Z[g] * mirror), c)
        return remote(z_send.at[e, g - 1], z_got.at[e, g - 1], reduce, 27 + e * 3 + g, to)

    def give_y(g, d):
        y_send[g, d - 1] = img_grad[at(img_slot(g, d)), :].astype(BF)
        go(cut_y(g, d))

    def give_core(g):
        core_send[g] = txt_grad[at(txt_slot(g, 1, 0), 4), :].astype(BF)
        go(cut_core(g))

    def give_x(g):
        cut_core(g).wait_recv()
        for d in (2, 1, 3):
            mine = txt_grad[at(txt_slot(g, 0, d)), :]
            x_send[g, d - 1] = (mine + core_got[g, at(d), :].astype(F32)).astype(BF)
            go(cut_x(g, d))
        return None

    def txt_total(g):
        total = txt_grad[at(txt_slot(g, 0, 0)), :] + core_got[g, at(0), :].astype(F32)
        for d in (1, 3, 2):
            cut_x(g, d).wait_recv()
            total += x_got[g, d - 1].astype(F32)
        return total

    def img_total(g):
        total = img_grad[at(img_slot(g, 0)), :]
        for d in (1, 3, 2):
            cut_y(g, d).wait_recv()
            total += y_got[g, d - 1].astype(F32)
        return total

    def give_z(e, g):
        z_send[e, g - 1] = (txt_total(g) if e else img_total(g)).astype(BF)
        go(cut_z(e, g))

    def swap_back(e, j):
        to = lax.rem(t + j, 4)
        out = (img_out, txt_out)[e]
        rows = pl.ds(pl.multiple_of(t * SHARD, SHARD), SHARD)
        return remote(back.at[e, to], out.at[rows], reduce, 34 + e * 3 + j - 1, (dp, to))

    def finish(e):
        total = txt_total(0) if e else img_total(0)
        for g in (1, 2, 3):
            cut_z(e, g).wait_recv()
            total += z_got[e, g - 1].astype(F32)
        rows, norm = unit(e)
        own = (txt[own_txt, :], img[own_img, :])[e].astype(F32)
        grad = scale * (total - own)
        inner = jnp.sum(rows * grad, axis=1, keepdims=True)
        grad = ((grad - rows * inner) / norm).astype(BF)
        for q in range(4):
            back[e, q] = grad[:, q * quarter : (q + 1) * quarter]
        for j in (2, 3, 1):
            go(swap_back(e, j))
        keep = pltpu.make_async_copy(
            back.at[e, t], (img_out, txt_out)[e].at[pl.ds(pl.multiple_of(t * SHARD, SHARD), SHARD)], in_sem.at[e]
        )
        keep.start()
        return keep

    for g in (1, 2, 3):
        img_z(g).wait_recv()
        for d in (2, 1, 3):
            go(img_y(g, d))
    forward_core(0)
    forward_x(2)
    forward_x(3)
    for g in range(4):
        for d in (1, 2, 3):
            img_y(g, d).wait_recv()
    forward_x(1)
    forward_core(2)
    got_core(2)
    pairs(2)
    give_core(2)
    forward_core(3)
    got_core(3)
    pairs(3)
    give_core(3)
    give_x(2)
    forward_core(1)
    give_x(3)
    got_core(1)
    pairs(1)
    give_core(1)
    got_core(0)
    for first in (0, 8):
        pairs(0, first, 8)
        give_x(1) if first == 0 else give_core(0)
        for slot in range(first, first + 8):
            if slot % 4:
                give_y(3 - slot // 4, slot % 4)
    give_z(1, 2)
    give_x(0)
    give_z(1, 3)
    give_z(1, 1)
    for g in (3, 2, 1):
        give_z(0, g)
    keep = [finish(0), finish(1)]
    for e in range(2):
        for j in (1, 2, 3):
            swap_back(e, j).wait_recv()
        keep[e].wait()
    for copy in sent:
        copy.wait_send()


def body(image_embed, text_embed, log_scale, logit_bias):
    rows, quarter = image_embed.shape
    width = 4 * quarter
    padded = 4 * SHARD
    vmem = pltpu.VMEM
    outs = pl.pallas_call(
        kernel,
        out_shape=[jax.ShapeDtypeStruct((padded, quarter), BF)] * 2,
        in_specs=[pl.BlockSpec(memory_space=pl.ANY)] * 4,
        out_specs=[pl.BlockSpec(memory_space=pl.ANY)] * 2,
        scratch_shapes=[
            pltpu.SMEM((1,), F32),
            pltpu.SMEM((1,), F32),
            vmem((2, padded, quarter), BF),
            vmem((2, 4, SHARD, quarter), BF),
            vmem((16 * SHARD, width), BF),
            vmem((32 * SHARD, width), BF),
            vmem((16 * SHARD, width), F32),
            vmem((32 * SHARD, width), F32),
            vmem((4, 4 * SHARD, width), BF),
            vmem((4, 4 * SHARD, width), BF),
            vmem((4, 3, SHARD, width), BF),
            vmem((4, 3, SHARD, width), BF),
            vmem((4, 3, SHARD, width), BF),
            vmem((4, 3, SHARD, width), BF),
            vmem((2, 3, SHARD, width), BF),
            vmem((2, 3, SHARD, width), BF),
            vmem((2, 4, SHARD, quarter), BF),
            pltpu.SemaphoreType.DMA((4,)),
            pltpu.SemaphoreType.DMA((53,)),
            pltpu.SemaphoreType.DMA((53,)),
            pltpu.SemaphoreType.DMA((40,)),
            pltpu.SemaphoreType.DMA((40,)),
        ],
        compiler_params=pltpu.CompilerParams(
            collective_id=0, has_side_effects=True, vmem_limit_bytes=56 * 2**20
        ),
    )(log_scale, logit_bias, image_embed, text_embed)
    return tuple(out[:rows].astype(F32) for out in outs)


def solution(mesh):
    placed = (P("dp", "tensor"), P("dp", "tensor"), P(), P())
    return jax.shard_map(
        body,
        mesh=mesh,
        in_specs=placed,
        out_specs=(P("dp", "tensor"), P("dp", "tensor")),
        check_vma=False,
    )
```

```python
import jax
import jax.numpy as jnp
from jax import lax
from jax.experimental import pallas as pl
from jax.experimental.pallas import tpu as pltpu
from jax.sharding import PartitionSpec as P

MESH = pl.DeviceIdType.MESH
BF = jnp.bfloat16
F32 = jnp.float32
NX, NY, NZ = 4, 4, 16
SHARD = 48
IMG_Z = (0, 1, -1, 2)
TXT_Z = (0, 8, 4, 12)
FIRST = 2
HALF = 640


def coords():
    dp, t = lax.axis_index("dp"), lax.axis_index("tensor")
    return (t // 2) * 2 + lax.rem(dp, 2), lax.rem(dp // 2, NY), dp // (2 * NY), lax.rem(t, 2)


def device(x, y, z, c):
    x, y, z = lax.rem(x + 2 * NX, NX), lax.rem(y + 2 * NY, NY), lax.rem(z + 2 * NZ, NZ)
    return (z * (2 * NY) + y * 2 + lax.rem(x, 2), (x // 2) * 2 + lax.rem(c, 2))


def at(slot, count=1):
    return pl.ds(slot * SHARD, count * SHARD)


def img_slot(g, d):
    return (3 - g) * 4 + d


def txt_slot(g, core, d):
    return g * 8 + core * 4 + d


def kernel(
    scale_in, bias_in, img_in, txt_in, img_out, txt_out,
    scale_ref, bias_ref, units, norms, block, raw, img, txt, img_grad, txt_grad,
    core_send, core_got, x_send, x_got, y_send, y_got, z_send, z_got, back,
    in_sem, gs, gr, rs, rr,
):
    x, y, z, c = coords()
    dp, t = lax.axis_index("dp"), lax.axis_index("tensor")
    quarter = block.shape[2]
    rows_in = img_in.shape[0]
    mirror = 1 - 2 * c

    loads = [
        pltpu.make_async_copy(ref, block.at[e, pl.ds(0, rows_in)], in_sem.at[e])
        for e, ref in enumerate((img_in, txt_in))
    ]
    loads.append(pltpu.make_async_copy(scale_in, scale_ref, in_sem.at[2]))
    loads.append(pltpu.make_async_copy(bias_in, bias_ref, in_sem.at[3]))
    for load in loads:
        load.start()
    for e in range(2):
        block[e, rows_in:, :] = jnp.zeros((block.shape[1] - rows_in, quarter), BF)

    peers = [(x, y, z + d, c) for d in (1, -1, 2, -2, 4, 8, 12)]
    peers += [(x, y + d, z, c) for d in (1, 2, 3)] + [(x + d, y, z, c) for d in (1, 2, 3)]
    peers += [(x, y, z, c + 1), (x + 2, y, z, c + 1)]
    barrier = pltpu.get_barrier_semaphore()
    for peer in peers:
        pl.semaphore_signal(barrier, inc=1, device_id=device(*peer), device_id_type=MESH)
    pl.semaphore_wait(barrier, len(peers))

    sent = []

    def go(copy):
        copy.start()
        sent.append(copy)

    def remote(src, dst, sems, index, to):
        return pltpu.make_async_remote_copy(
            src_ref=src, dst_ref=dst, send_sem=sems[0].at[index], recv_sem=sems[1].at[index],
            device_id=to, device_id_type=MESH,
        )

    gather, reduce = (gs, gr), (rs, rr)

    def swap(e, j):
        to = lax.rem(t + j, 4)
        rows = pl.ds(pl.multiple_of(to * SHARD, SHARD), SHARD)
        return remote(block.at[e, rows], raw.at[e, t], gather, e * 3 + j - 1, (dp, to))

    for e in (0, 1):
        loads[e].wait()
        for j in (2, 3, 1):
            go(swap(e, j))
        raw[e, t] = block[e, pl.ds(pl.multiple_of(t * SHARD, SHARD), SHARD), :]

    def unit(e):
        rows = jnp.concatenate([raw[e, q].astype(F32) for q in range(4)], axis=1)
        norm = jnp.sqrt(jnp.sum(rows * rows, axis=1, keepdims=True) + 1e-06)
        units[e] = rows / norm
        norms[e] = jnp.broadcast_to(norm, norms.shape[1:])
        return units[e].astype(BF)

    def txt_z(g):
        to = device(x, y, z + TXT_Z[g], c)
        return remote(txt.at[at(0)], txt.at[at(txt_slot(g, 0, 0))], gather, 5 + g, to)

    def txt_far(h):
        lanes = (pl.ds(0, HALF), pl.ds(HALF, txt.shape[1] - HALF))[h]
        to = device(x, y, z + (4, -4)[h], c)
        src, dst = txt.at[at(txt_slot(2 + h, 0, 0)), lanes], txt.at[at(txt_slot(1, 0, 0)), lanes]
        return remote(src, dst, gather, (6, 52)[h], to)

    def txt_x(g, d):
        to = device(x + d, y, z, c)
        return remote(txt.at[at(txt_slot(g, 0, 0))], txt.at[at(txt_slot(g, 0, d))], gather, 8 + g * 3 + d, to)

    def txt_core(g, d):
        to = device(x, y, z, c + 1)
        return remote(txt.at[at(txt_slot(g, 0, d))], txt.at[at(txt_slot(g, 1, d))], gather, 21 + g * 4 + d, to)

    def img_z(g):
        to = device(x, y, z + IMG_Z[g] * mirror, c)
        return remote(img.at[at(img_slot(0, 0))], img.at[at(img_slot(g, 0))], gather, 36 + g, to)

    def img_y(g, d):
        to = device(x, y + d, z, c)
        return remote(img.at[at(img_slot(g, 0))], img.at[at(img_slot(g, d))], gather, 39 + g * 3 + d, to)

    own_img, own_txt = at(img_slot(0, 0)), at(txt_slot(0, 0, 0))
    for j in (1, 3, 2):
        swap(0, j).wait_recv()
    img[own_img, :] = unit(0)
    for g in (3, 1, 2):
        go(img_z(g))
    for d in (2, 1, 3):
        go(img_y(0, d))
    for j in (1, 3, 2):
        swap(1, j).wait_recv()
    txt[own_txt, :] = unit(1)
    for g in (2, 3):
        go(txt_z(g))
    for d in (2, 1, 3):
        go(txt_x(0, d))
    go(txt_core(0, 0))

    for load in loads[2:]:
        load.wait()
    scale = jnp.exp(jnp.full((1, 1), scale_ref[0], F32))
    bias = bias_ref[0]

    def forward_x(g):
        if g == 1:
            txt_far(0).wait_recv()
            txt_far(1).wait_recv()
        else:
            txt_z(g).wait_recv()
            go(txt_far(g - 2))
        for d in (2, 1, 3):
            go(txt_x(g, d))
        go(txt_core(g, 0))

    def forward_core(g):
        for d in (1, 3, 2):
            txt_x(g, d).wait_recv()
            go(txt_core(g, d))

    def got_core(g):
        for d in range(4):
            txt_core(g, d).wait_recv()

    def pairs(g, first=0, count=16):
        here, there = at(txt_slot(g, 0, 0), 8), at(first, count)
        scores = lax.dot_general(
            img[there, :], txt[here, :], (((1,), (1,)), ((), ())), preferred_element_type=F32
        )
        part = jax.nn.sigmoid(scale * scores + bias).astype(BF)
        to_img = jnp.dot(part, txt[here, :], preferred_element_type=F32)
        if g == FIRST:
            img_grad[there, :] = to_img
        else:
            img_grad[there, :] += to_img
        to_txt = lax.dot_general(part, img[there, :], (((0,), (0,)), ((), ())), preferred_element_type=F32)
        if first == 0:
            txt_grad[here, :] = to_txt
        else:
            txt_grad[here, :] += to_txt

    def cut_core(g):
        to = device(x, y, z, c + 1)
        return remote(core_send.at[g], core_got.at[g], reduce, g, to)

    def cut_x(g, d):
        to = device(x - d, y, z, c)
        return remote(x_send.at[g, d - 1], x_got.at[g, d - 1], reduce, 3 + g * 3 + d, to)

    def cut_y(g, d):
        to = device(x, y - d, z, c)
        return remote(y_send.at[g, d - 1], y_got.at[g, d - 1], reduce, 15 + g * 3 + d, to)

    def cut_z(e, g):
        to = device(x, y, z - (TXT_Z[g] if e else IMG_Z[g] * mirror), c)
        return remote(z_send.at[e, g - 1], z_got.at[e, g - 1], reduce, 27 + e * 3 + g, to)

    def give_y(g, d):
        y_send[g, d - 1] = img_grad[at(img_slot(g, d)), :].astype(BF)
        go(cut_y(g, d))

    def give_core(g):
        core_send[g] = txt_grad[at(txt_slot(g, 1, 0), 4), :].astype(BF)
        go(cut_core(g))

    def give_x(g):
        cut_core(g).wait_recv()
        for d in (2, 1, 3):
            mine = txt_grad[at(txt_slot(g, 0, d)), :]
            x_send[g, d - 1] = (mine + core_got[g, at(d), :].astype(F32)).astype(BF)
            go(cut_x(g, d))
        return None

    def txt_total(g):
        total = txt_grad[at(txt_slot(g, 0, 0)), :] + core_got[g, at(0), :].astype(F32)
        for d in (1, 3, 2):
            cut_x(g, d).wait_recv()
            total += x_got[g, d - 1].astype(F32)
        return total

    def img_total(g):
        total = img_grad[at(img_slot(g, 0)), :]
        for d in (1, 3, 2):
            cut_y(g, d).wait_recv()
            total += y_got[g, d - 1].astype(F32)
        return total

    def give_z(e, g):
        z_send[e, g - 1] = (txt_total(g) if e else img_total(g)).astype(BF)
        go(cut_z(e, g))

    def swap_back(e, j):
        to = lax.rem(t + j, 4)
        out = (img_out, txt_out)[e]
        rows = pl.ds(pl.multiple_of(t * SHARD, SHARD), SHARD)
        return remote(back.at[e, to], out.at[rows], reduce, 34 + e * 3 + j - 1, (dp, to))

    def finish(e):
        total = txt_total(0) if e else img_total(0)
        for g in (1, 2, 3):
            cut_z(e, g).wait_recv()
            total += z_got[e, g - 1].astype(F32)
        rows, norm = units[e], norms[e, :, :1]
        own = (txt[own_txt, :], img[own_img, :])[e].astype(F32)
        grad = scale * (total - own)
        inner = jnp.sum(rows * grad, axis=1, keepdims=True)
        grad = ((grad - rows * inner) / norm).astype(BF)
        for q in range(4):
            back[e, q] = grad[:, q * quarter : (q + 1) * quarter]
        for j in (2, 3, 1):
            go(swap_back(e, j))
        keep = pltpu.make_async_copy(
            back.at[e, t], (img_out, txt_out)[e].at[pl.ds(pl.multiple_of(t * SHARD, SHARD), SHARD)], in_sem.at[e]
        )
        keep.start()
        return keep

    for g in (1, 2, 3):
        img_z(g).wait_recv()
        for d in (2, 1, 3):
            go(img_y(g, d))
    forward_core(0)
    forward_x(2)
    forward_x(3)
    forward_x(1)
    forward_core(2)
    for g in range(4):
        for d in (1, 2, 3):
            img_y(g, d).wait_recv()
    got_core(2)
    pairs(2)
    give_core(2)
    forward_core(3)
    got_core(3)
    pairs(3)
    give_core(3)
    give_x(2)
    forward_core(1)
    give_x(3)
    got_core(0)
    pairs(0, 0, 8)
    got_core(1)
    pairs(1)
    give_core(1)
    for first in (0, 8):
        if first:
            give_x(1)
            pairs(0, first, 8)
            give_core(0)
        for slot in range(first, first + 8):
            if slot % 4:
                give_y(3 - slot // 4, slot % 4)
    give_z(1, 2)
    give_x(0)
    give_z(1, 3)
    give_z(1, 1)
    for g in (3, 2, 1):
        give_z(0, g)
    keep = [finish(0), finish(1)]
    for e in range(2):
        for j in (1, 2, 3):
            swap_back(e, j).wait_recv()
        keep[e].wait()
    for copy in sent:
        copy.wait_send()


def body(image_embed, text_embed, log_scale, logit_bias):
    rows, quarter = image_embed.shape
    width = 4 * quarter
    padded = 4 * SHARD
    vmem = pltpu.VMEM
    outs = pl.pallas_call(
        kernel,
        out_shape=[jax.ShapeDtypeStruct((padded, quarter), BF)] * 2,
        in_specs=[pl.BlockSpec(memory_space=pl.ANY)] * 4,
        out_specs=[pl.BlockSpec(memory_space=pl.ANY)] * 2,
        scratch_shapes=[
            pltpu.SMEM((1,), F32),
            pltpu.SMEM((1,), F32),
            vmem((2, SHARD, width), F32),
            vmem((2, SHARD, 128), F32),
            vmem((2, padded, quarter), BF),
            vmem((2, 4, SHARD, quarter), BF),
            vmem((16 * SHARD, width), BF),
            vmem((32 * SHARD, width), BF),
            vmem((16 * SHARD, width), F32),
            vmem((32 * SHARD, width), F32),
            vmem((4, 4 * SHARD, width), BF),
            vmem((4, 4 * SHARD, width), BF),
            vmem((4, 3, SHARD, width), BF),
            vmem((4, 3, SHARD, width), BF),
            vmem((4, 3, SHARD, width), BF),
            vmem((4, 3, SHARD, width), BF),
            vmem((2, 3, SHARD, width), BF),
            vmem((2, 3, SHARD, width), BF),
            vmem((2, 4, SHARD, quarter), BF),
            pltpu.SemaphoreType.DMA((4,)),
            pltpu.SemaphoreType.DMA((53,)),
            pltpu.SemaphoreType.DMA((53,)),
            pltpu.SemaphoreType.DMA((40,)),
            pltpu.SemaphoreType.DMA((40,)),
        ],
        compiler_params=pltpu.CompilerParams(
            collective_id=0, has_side_effects=True, vmem_limit_bytes=56 * 2**20
        ),
    )(log_scale, logit_bias, image_embed, text_embed)
    return tuple(out[:rows].astype(F32) for out in outs)


def solution(mesh):
    placed = (P("dp", "tensor"), P("dp", "tensor"), P(), P())
    return jax.shard_map(
        body,
        mesh=mesh,
        in_specs=placed,
        out_specs=(P("dp", "tensor"), P("dp", "tensor")),
        check_vma=False,
    )
```

```python
import jax
import jax.numpy as jnp
from jax import lax
from jax.experimental import pallas as pl
from jax.experimental.pallas import tpu as pltpu
from jax.sharding import PartitionSpec as P

MESH = pl.DeviceIdType.MESH
BF = jnp.bfloat16
F32 = jnp.float32
NX, NY, NZ = 4, 4, 16
SHARD = 48
IMG_Z = (0, 1, -1, 2)
TXT_Z = (0, 8, 4, 12)
FIRST = 2
HALF = 640


def coords():
    dp, t = lax.axis_index("dp"), lax.axis_index("tensor")
    return (t // 2) * 2 + lax.rem(dp, 2), lax.rem(dp // 2, NY), dp // (2 * NY), lax.rem(t, 2)


def device(x, y, z, c):
    x, y, z = lax.rem(x + 2 * NX, NX), lax.rem(y + 2 * NY, NY), lax.rem(z + 2 * NZ, NZ)
    return (z * (2 * NY) + y * 2 + lax.rem(x, 2), (x // 2) * 2 + lax.rem(c, 2))


def at(slot, count=1):
    return pl.ds(slot * SHARD, count * SHARD)


def img_slot(g, d):
    return (3 - g) * 4 + d


def txt_slot(g, core, d):
    return g * 8 + core * 4 + d


def kernel(
    scale_in, bias_in, img_in, txt_in, img_out, txt_out,
    scale_ref, bias_ref, units, norms, block, raw, img, txt, img_grad, txt_grad,
    core_send, core_got, x_send, x_got, y_send, y_got, z_send, z_got, back,
    in_sem, gs, gr, rs, rr,
):
    x, y, z, c = coords()
    dp, t = lax.axis_index("dp"), lax.axis_index("tensor")
    quarter = block.shape[2]
    rows_in = img_in.shape[0]
    mirror = 1 - 2 * c

    loads = [
        pltpu.make_async_copy(ref, block.at[e, pl.ds(0, rows_in)], in_sem.at[e])
        for e, ref in enumerate((img_in, txt_in))
    ]
    loads.append(pltpu.make_async_copy(scale_in, scale_ref, in_sem.at[2]))
    loads.append(pltpu.make_async_copy(bias_in, bias_ref, in_sem.at[3]))
    for load in loads:
        load.start()
    for e in range(2):
        block[e, rows_in:, :] = jnp.zeros((block.shape[1] - rows_in, quarter), BF)

    peers = [(x, y, z + d, c) for d in (1, -1, 2, -2, 4, 8, 12)]
    peers += [(x, y + d, z, c) for d in (1, 2, 3)] + [(x + d, y, z, c) for d in (1, 2, 3)]
    peers += [(x, y, z, c + 1), (x + 2, y, z, c + 1)]
    barrier = pltpu.get_barrier_semaphore()
    for peer in peers:
        pl.semaphore_signal(barrier, inc=1, device_id=device(*peer), device_id_type=MESH)
    pl.semaphore_wait(barrier, len(peers))

    sent = []

    def go(copy):
        copy.start()
        sent.append(copy)

    def remote(src, dst, sems, index, to):
        return pltpu.make_async_remote_copy(
            src_ref=src, dst_ref=dst, send_sem=sems[0].at[index], recv_sem=sems[1].at[index],
            device_id=to, device_id_type=MESH,
        )

    gather, reduce = (gs, gr), (rs, rr)

    def swap(e, j):
        to = lax.rem(t + j, 4)
        rows = pl.ds(pl.multiple_of(to * SHARD, SHARD), SHARD)
        return remote(block.at[e, rows], raw.at[e, t], gather, e * 3 + j - 1, (dp, to))

    for e in (0, 1):
        loads[e].wait()
        for j in (2, 3, 1):
            go(swap(e, j))
        raw[e, t] = block[e, pl.ds(pl.multiple_of(t * SHARD, SHARD), SHARD), :]

    def unit(e):
        rows = jnp.concatenate([raw[e, q].astype(F32) for q in range(4)], axis=1)
        norm = jnp.sqrt(jnp.sum(rows * rows, axis=1, keepdims=True) + 1e-06)
        units[e] = rows / norm
        norms[e] = jnp.broadcast_to(norm, norms.shape[1:])
        return units[e].astype(BF)

    def txt_z(g):
        to = device(x, y, z + TXT_Z[g], c)
        return remote(txt.at[at(0)], txt.at[at(txt_slot(g, 0, 0))], gather, 5 + g, to)

    def txt_far(h):
        lanes = (pl.ds(0, HALF), pl.ds(HALF, txt.shape[1] - HALF))[h]
        to = device(x, y, z + (4, -4)[h], c)
        src, dst = txt.at[at(txt_slot(2 + h, 0, 0)), lanes], txt.at[at(txt_slot(1, 0, 0)), lanes]
        return remote(src, dst, gather, (6, 52)[h], to)

    def txt_x(g, d):
        to = device(x + d, y, z, c)
        return remote(txt.at[at(txt_slot(g, 0, 0))], txt.at[at(txt_slot(g, 0, d))], gather, 8 + g * 3 + d, to)

    def txt_core(g, d):
        to = device(x, y, z, c + 1)
        return remote(txt.at[at(txt_slot(g, 0, d))], txt.at[at(txt_slot(g, 1, d))], gather, 21 + g * 4 + d, to)

    def img_z(g):
        to = device(x, y, z + IMG_Z[g] * mirror, c)
        return remote(img.at[at(img_slot(0, 0))], img.at[at(img_slot(g, 0))], gather, 36 + g, to)

    def img_y(g, d):
        to = device(x, y + d, z, c)
        return remote(img.at[at(img_slot(g, 0))], img.at[at(img_slot(g, d))], gather, 39 + g * 3 + d, to)

    def img_far(g, h):
        lanes = (pl.ds(0, HALF), pl.ds(HALF, img.shape[1] - HALF))[h]
        to = device(x, y + (1, -1)[h], z, c)
        src, dst = img.at[at(img_slot(g, (1, 3)[h])), lanes], img.at[at(img_slot(g, 2)), lanes]
        return remote(src, dst, gather, (41 + g * 3, 53 + g)[h], to)

    def forward_y(g):
        for h, d in enumerate((1, 3)):
            img_y(g, d).wait_recv()
            go(img_far(g, h))

    own_img, own_txt = at(img_slot(0, 0)), at(txt_slot(0, 0, 0))
    for j in (1, 3, 2):
        swap(0, j).wait_recv()
    img[own_img, :] = unit(0)
    for g in (3, 1, 2):
        go(img_z(g))
    for d in (1, 3):
        go(img_y(0, d))
    for j in (1, 3, 2):
        swap(1, j).wait_recv()
    txt[own_txt, :] = unit(1)
    for g in (2, 3):
        go(txt_z(g))
    for d in (2, 1, 3):
        go(txt_x(0, d))
    go(txt_core(0, 0))

    for load in loads[2:]:
        load.wait()
    scale = jnp.exp(jnp.full((1, 1), scale_ref[0], F32))
    bias = bias_ref[0]

    def forward_x(g):
        if g == 1:
            txt_far(0).wait_recv()
            txt_far(1).wait_recv()
        else:
            txt_z(g).wait_recv()
            go(txt_far(g - 2))
        for d in (2, 1, 3):
            go(txt_x(g, d))
        go(txt_core(g, 0))

    def forward_core(g):
        for d in (1, 3, 2):
            txt_x(g, d).wait_recv()
            go(txt_core(g, d))

    def got_core(g):
        for d in range(4):
            txt_core(g, d).wait_recv()

    def pairs(g, first=0, count=16):
        here, there = at(txt_slot(g, 0, 0), 8), at(first, count)
        scores = lax.dot_general(
            img[there, :], txt[here, :], (((1,), (1,)), ((), ())), preferred_element_type=F32
        )
        part = jax.nn.sigmoid(scale * scores + bias).astype(BF)
        to_img = jnp.dot(part, txt[here, :], preferred_element_type=F32)
        if g == FIRST:
            img_grad[there, :] = to_img
        else:
            img_grad[there, :] += to_img
        to_txt = lax.dot_general(part, img[there, :], (((0,), (0,)), ((), ())), preferred_element_type=F32)
        if first == 0:
            txt_grad[here, :] = to_txt
        else:
            txt_grad[here, :] += to_txt

    def cut_core(g):
        to = device(x, y, z, c + 1)
        return remote(core_send.at[g], core_got.at[g], reduce, g, to)

    def cut_x(g, d):
        to = device(x - d, y, z, c)
        return remote(x_send.at[g, d - 1], x_got.at[g, d - 1], reduce, 3 + g * 3 + d, to)

    def cut_y(g, d):
        to = device(x, y - d, z, c)
        return remote(y_send.at[g, d - 1], y_got.at[g, d - 1], reduce, 15 + g * 3 + d, to)

    def cut_z(e, g):
        to = device(x, y, z - (TXT_Z[g] if e else IMG_Z[g] * mirror), c)
        return remote(z_send.at[e, g - 1], z_got.at[e, g - 1], reduce, 27 + e * 3 + g, to)

    def give_y(g, d):
        y_send[g, d - 1] = img_grad[at(img_slot(g, d)), :].astype(BF)
        go(cut_y(g, d))

    def give_core(g):
        core_send[g] = txt_grad[at(txt_slot(g, 1, 0), 4), :].astype(BF)
        go(cut_core(g))

    def give_x(g):
        cut_core(g).wait_recv()
        for d in (2, 1, 3):
            mine = txt_grad[at(txt_slot(g, 0, d)), :]
            x_send[g, d - 1] = (mine + core_got[g, at(d), :].astype(F32)).astype(BF)
            go(cut_x(g, d))
        return None

    def txt_total(g):
        total = txt_grad[at(txt_slot(g, 0, 0)), :] + core_got[g, at(0), :].astype(F32)
        for d in (1, 3, 2):
            cut_x(g, d).wait_recv()
            total += x_got[g, d - 1].astype(F32)
        return total

    def img_total(g):
        total = img_grad[at(img_slot(g, 0)), :]
        for d in (1, 3, 2):
            cut_y(g, d).wait_recv()
            total += y_got[g, d - 1].astype(F32)
        return total

    def give_z(e, g):
        z_send[e, g - 1] = (txt_total(g) if e else img_total(g)).astype(BF)
        go(cut_z(e, g))

    def swap_back(e, j):
        to = lax.rem(t + j, 4)
        out = (img_out, txt_out)[e]
        rows = pl.ds(pl.multiple_of(t * SHARD, SHARD), SHARD)
        return remote(back.at[e, to], out.at[rows], reduce, 34 + e * 3 + j - 1, (dp, to))

    def finish(e):
        total = txt_total(0) if e else img_total(0)
        for g in (1, 2, 3):
            cut_z(e, g).wait_recv()
            total += z_got[e, g - 1].astype(F32)
        rows, norm = units[e], norms[e, :, :1]
        own = (txt[own_txt, :], img[own_img, :])[e].astype(F32)
        grad = scale * (total - own)
        inner = jnp.sum(rows * grad, axis=1, keepdims=True)
        grad = ((grad - rows * inner) / norm).astype(BF)
        for q in range(4):
            back[e, q] = grad[:, q * quarter : (q + 1) * quarter]
        for j in (2, 3, 1):
            go(swap_back(e, j))
        keep = pltpu.make_async_copy(
            back.at[e, t], (img_out, txt_out)[e].at[pl.ds(pl.multiple_of(t * SHARD, SHARD), SHARD)], in_sem.at[e]
        )
        keep.start()
        return keep

    for g in (1, 2, 3):
        img_z(g).wait_recv()
        for d in (1, 3):
            go(img_y(g, d))
    forward_y(0)
    forward_core(0)
    forward_x(2)
    forward_x(3)
    for g in (1, 2, 3):
        forward_y(g)
    forward_x(1)
    forward_core(2)
    for g in range(4):
        for h in range(2):
            img_far(g, h).wait_recv()
    got_core(2)
    pairs(2)
    give_core(2)
    forward_core(3)
    got_core(3)
    pairs(3)
    give_core(3)
    give_x(2)
    forward_core(1)
    give_x(3)
    got_core(0)
    pairs(0, 0, 8)
    got_core(1)
    pairs(1)
    give_core(1)
    for first in (0, 8):
        if first:
            give_x(1)
            pairs(0, first, 8)
            give_core(0)
        for slot in range(first, first + 8):
            if slot % 4:
                give_y(3 - slot // 4, slot % 4)
    give_z(1, 2)
    give_x(0)
    give_z(1, 3)
    give_z(1, 1)
    for g in (3, 2, 1):
        give_z(0, g)
    keep = [finish(0), finish(1)]
    for e in range(2):
        for j in (1, 2, 3):
            swap_back(e, j).wait_recv()
        keep[e].wait()
    for copy in sent:
        copy.wait_send()


def body(image_embed, text_embed, log_scale, logit_bias):
    rows, quarter = image_embed.shape
    width = 4 * quarter
    padded = 4 * SHARD
    vmem = pltpu.VMEM
    outs = pl.pallas_call(
        kernel,
        out_shape=[jax.ShapeDtypeStruct((padded, quarter), BF)] * 2,
        in_specs=[pl.BlockSpec(memory_space=pl.ANY)] * 4,
        out_specs=[pl.BlockSpec(memory_space=pl.ANY)] * 2,
        scratch_shapes=[
            pltpu.SMEM((1,), F32),
            pltpu.SMEM((1,), F32),
            vmem((2, SHARD, width), F32),
            vmem((2, SHARD, 128), F32),
            vmem((2, padded, quarter), BF),
            vmem((2, 4, SHARD, quarter), BF),
            vmem((16 * SHARD, width), BF),
            vmem((32 * SHARD, width), BF),
            vmem((16 * SHARD, width), F32),
            vmem((32 * SHARD, width), F32),
            vmem((4, 4 * SHARD, width), BF),
            vmem((4, 4 * SHARD, width), BF),
            vmem((4, 3, SHARD, width), BF),
            vmem((4, 3, SHARD, width), BF),
            vmem((4, 3, SHARD, width), BF),
            vmem((4, 3, SHARD, width), BF),
            vmem((2, 3, SHARD, width), BF),
            vmem((2, 3, SHARD, width), BF),
            vmem((2, 4, SHARD, quarter), BF),
            pltpu.SemaphoreType.DMA((4,)),
            pltpu.SemaphoreType.DMA((57,)),
            pltpu.SemaphoreType.DMA((57,)),
            pltpu.SemaphoreType.DMA((40,)),
            pltpu.SemaphoreType.DMA((40,)),
        ],
        compiler_params=pltpu.CompilerParams(
            collective_id=0, has_side_effects=True, vmem_limit_bytes=56 * 2**20
        ),
    )(log_scale, logit_bias, image_embed, text_embed)
    return tuple(out[:rows].astype(F32) for out in outs)


def solution(mesh):
    placed = (P("dp", "tensor"), P("dp", "tensor"), P(), P())
    return jax.shard_map(
        body,
        mesh=mesh,
        in_specs=placed,
        out_specs=(P("dp", "tensor"), P("dp", "tensor")),
        check_vma=False,
    )
```
